512 devices in a mesh: blk: 128 (over y_lo, x, z), pair: 4 (over y_hi, core).
Axes of the slice: x: 4, y: 4 (y_hi: 2, y_lo: 2; y = y_hi * 2 + y_lo), z: 16, core: 2. Of those that a mesh axis runs over, the one named last changes fastest.
Arguments:
- points: bfloat16 [16, 1048576], P(None, ('blk', 'pair')), may hold values from -6 to 6
- values: bfloat16 [8, 1048576], P(None, ('blk', 'pair')), may hold values from -0.5 to 0.5
- length_scales: float32 [16], replicated, may hold values from 1.5 to 6
- partners: int32 [2, 128], P(None, 'blk'), may hold values from 0 to 127, as said below
Outputs:
- product: float32 [8, 1048576], P(None, ('blk', 'pair'))
The draws below stay inside these ranges and needn't reach their ends.
Inputs may be any that keep to these rules, and one draw needn't show every extreme that they name: In round r every block b is paired with b XOR m_r, where m_r is a nonzero mask shared by all blocks of that round and different from the other rounds' masks; so partners[r, partners[r, b]] = b.
All inputs are finite; a program needn't handle non-finite values.
Results may differ from the reference program's by a relative error of at most 0.003.
Values may be sent and summed in bfloat16 or wider, within the bound.
No kernel may reach another device: no remote copies, remote signals or barrier semaphores. Data moves between devices by JAX's collectives and lax.ppermute only.
A program may use at most 64 MiB of HBM per device.

```python
import math
import jax
import jax.numpy as jnp
from jax import lax

FEATURES = 16
RHS = 8
ROUNDS = 2
BLOCKS = 128
BLOCK = 8192
NPTS = 1048576


def draw_partners(key, part):
    key = jax.random.fold_in(key, 11)
    chosen = jax.random.permutation(key, BLOCKS - 1)[:ROUNDS].astype(jnp.int32) + 1
    block_ids = jnp.arange(BLOCKS, dtype=jnp.int32)
    return jnp.bitwise_xor(block_ids[None, :], chosen[:, None])


def level_of(stream_key, dims, cuts, least, top_value):
    def one(position, blocks):
        steps = jax.random.uniform(jax.random.fold_in(jax.random.fold_in(stream_key, 6), position), (blocks,), jnp.float32, least / len(cuts), top_value / len(cuts))
        return jnp.repeat(jnp.exp(steps), dims[position] // blocks).reshape((-1,) + (1,) * (len(dims) - position - 1))

    level = one(*cuts[0])
    for cut in cuts[1:]:
        level = level * one(*cut)
    return level


def normal_values(own_key, shape, scale, limit, split=(), held_as=jnp.bfloat16):
    result = jax.random.normal(own_key, shape, jnp.float32) * scale
    if len(split) > 0:
        result = level_of(own_key, shape, split, -0.22, 0.18) * result
    return jnp.clip(result, min=-limit, max=limit).astype(held_as)


def setup_inputs(seed: int = 0) -> dict:
    arg_keys = jax.random.split(jax.random.key(seed), 5)
    return {
        "points": normal_values(arg_keys[0], (FEATURES, NPTS), 1.0, 6.0, ((1, 512),)),
        "values": normal_values(arg_keys[1], (RHS, NPTS), (4.0 * (ROUNDS * BLOCK) ** -0.5), 0.5, ((1, 512),)),
        "length_scales": jnp.clip(jnp.exp(jax.random.uniform(arg_keys[2], (FEATURES,), jnp.float32, math.log(1.5), math.log(6.0))), 1.5, 6.0),
        "partners": draw_partners(jax.random.fold_in(arg_keys[4], 71), 0),
    }


def gauss_tile(row_scaled, row_sq, col_scaled, col_sq):
    cross_dot = lax.dot_general(row_scaled, col_scaled, (((0,), (0,)), ((), ())), precision=lax.Precision.HIGHEST, preferred_element_type=jnp.float32)
    return jnp.exp(-0.5 * (row_sq[:, None] + col_sq[None, :] - 2.0 * cross_dot)).astype(jnp.bfloat16)


def reference(points, values, length_scales, partners):
    scaled = points.astype(jnp.float32) / length_scales[:, None]
    sq_norms = jnp.sum(scaled * scaled, axis=0)

    def one_block(block_index):
        block_start = (block_index * BLOCK).astype(jnp.int32)
        own_scaled = lax.dynamic_slice_in_dim(scaled, block_start, BLOCK, 1)
        own_sq = lax.dynamic_slice_in_dim(sq_norms, block_start, BLOCK, 0)

        def one_round(running, round_index):
            far_block = partners[round_index, block_index]
            far_start = (far_block * BLOCK).astype(jnp.int32)
            far_scaled = lax.dynamic_slice_in_dim(scaled, far_start, BLOCK, 1)
            far_sq = lax.dynamic_slice_in_dim(sq_norms, far_start, BLOCK, 0)
            far_vals = lax.dynamic_slice_in_dim(values, far_start, BLOCK, 1)
            kernel = gauss_tile(far_scaled, far_sq, own_scaled, own_sq)
            return running + jnp.dot(far_vals, kernel, preferred_element_type=jnp.float32), None

        running, _ = lax.scan(one_round, jnp.zeros((RHS, BLOCK), jnp.float32), jnp.arange(ROUNDS, dtype=jnp.int32))
        return running

    blocks_out = lax.map(one_block, jnp.arange(BLOCKS, dtype=jnp.int32))
    return jnp.transpose(blocks_out, (1, 0, 2)).reshape(RHS, BLOCKS * BLOCK)
```

```python
import functools
import math

import jax
import jax.numpy as jnp
from jax import lax
from jax.experimental import pallas as pl
from jax.experimental.pallas import tpu as pltpu
from jax.sharding import PartitionSpec as P

LOG2E = math.log2(math.e)
DEPTH = 64
ROW_TILE = 1024


def split3(x):
    high = x.astype(jnp.bfloat16)
    rest = x - high.astype(jnp.float32)
    mid = rest.astype(jnp.bfloat16)
    low = (rest - mid.astype(jnp.float32)).astype(jnp.bfloat16)
    return high, mid, low


def half_norm(pts, inv_sq):
    return jnp.sum(pts * pts * inv_sq, axis=0, keepdims=True) * (-0.5 * LOG2E)


def norm_rows(own_first, norm):
    pieces = [p.astype(jnp.float32) for p in split3(norm)]
    row = lax.broadcasted_iota(jnp.int32, (16, norm.shape[1]), 0)
    start = 0 if own_first else 3
    other = 3 - start
    out = jnp.where((row >= other) & (row < other + 3), 1.0, 0.0)
    for i, piece in enumerate(pieces):
        out = jnp.where(row == start + i, piece, out)
    return out.astype(jnp.bfloat16)


def product_kernel(own_ref, ls_ref, far_ref, out_ref, own_side, far_side, far_rows):
    rounds, quarters, _, count = far_ref.shape
    scale = ls_ref[...]
    inv_sq = 1.0 / (scale * scale)
    own = own_ref[...].astype(jnp.float32)
    for i, piece in enumerate(split3(own * (inv_sq * LOG2E))):
        own_side[16 * i : 16 * i + 16, :] = piece
    own_side[48:64, :] = norm_rows(True, half_norm(own, inv_sq))
    out_ref[...] = jnp.zeros_like(out_ref)

    def step(index, carry):
        data = far_ref.at[index // quarters, index % quarters]
        raw = data[0:16, :]
        for i in range(3):
            far_side[16 * i : 16 * i + 16, :] = raw
        far_side[48:64, :] = norm_rows(False, half_norm(raw.astype(jnp.float32), inv_sq))
        far_rows[...] = far_side[...].T

        def tile(part, total):
            first = pl.multiple_of(part * ROW_TILE, ROW_TILE)
            power = jnp.dot(
                far_rows[pl.ds(first, ROW_TILE), :], own_side[...], preferred_element_type=jnp.float32
            )
            block = jnp.exp2(power).astype(jnp.bfloat16)
            vals = data[16:24, pl.ds(first, ROW_TILE)]
            return total + jnp.dot(vals, block, preferred_element_type=jnp.float32)

        out_ref[...] = lax.fori_loop(0, count // ROW_TILE, tile, out_ref[...])
        return carry

    lax.fori_loop(0, rounds * quarters, step, 0)


def block_product(own, scales, far):
    count = own.shape[1]
    return pl.pallas_call(
        product_kernel,
        out_shape=jax.ShapeDtypeStruct((8, count), jnp.float32),
        scratch_shapes=[
            pltpu.VMEM((DEPTH, count), jnp.bfloat16),
            pltpu.VMEM((DEPTH, count), jnp.bfloat16),
            pltpu.VMEM((count, DEPTH), jnp.bfloat16),
        ],
        compiler_params=pltpu.CompilerParams(vmem_limit_bytes=48 << 20),
    )(own, scales, far)


def move(mask, shard):
    return lax.ppermute(shard, "blk", [(i, i ^ mask) for i in range(lax.axis_size("blk"))])


def shards(points, values, length_scales, partners):
    blocks = lax.axis_size("blk")
    masks = jnp.bitwise_xor(partners[:, 0], lax.axis_index("blk"))
    mine = jnp.concatenate([points, values], 0)
    branches = [functools.partial(move, mask) for mask in range(blocks)]
    far = jnp.stack([lax.switch(masks[r], branches, mine) for r in range(partners.shape[0])])
    far = lax.all_gather(far, "pair", axis=1)
    return block_product(points, length_scales[:, None], far)


def solution(mesh):
    placed = (P(None, ("blk", "pair")), P(None, ("blk", "pair")), P(), P(None, "blk"))
    return jax.shard_map(
        shards, mesh=mesh, in_specs=placed, out_specs=P(None, ("blk", "pair")), check_vma=False
    )
```

```python
import functools
import math

import jax
import jax.numpy as jnp
from jax import lax
from jax.experimental import pallas as pl
from jax.experimental.pallas import tpu as pltpu
from jax.sharding import PartitionSpec as P

LOG2E = math.log2(math.e)
DEPTH = 64
ROW_TILE = 1024


def split3(x):
    high = x.astype(jnp.bfloat16)
    rest = x - high.astype(jnp.float32)
    mid = rest.astype(jnp.bfloat16)
    low = (rest - mid.astype(jnp.float32)).astype(jnp.bfloat16)
    return high, mid, low


def half_norm(pts, inv_sq):
    return jnp.sum(pts * pts * inv_sq, axis=0, keepdims=True) * (-0.5 * LOG2E)


def norm_rows(own_first, norm):
    pieces = [p.astype(jnp.float32) for p in split3(norm)]
    row = lax.broadcasted_iota(jnp.int32, (16, norm.shape[1]), 0)
    start = 0 if own_first else 3
    other = 3 - start
    out = jnp.where((row >= other) & (row < other + 3), 1.0, 0.0)
    for i, piece in enumerate(pieces):
        out = jnp.where(row == start + i, piece, out)
    return out.astype(jnp.bfloat16)


def product_kernel(own_ref, ls_ref, far_ref, out_ref, own_side, far_side, far_rows):
    rounds, quarters, _, count = far_ref.shape
    scale = ls_ref[...]
    inv_sq = 1.0 / (scale * scale)
    own = own_ref[...].astype(jnp.float32)
    for i, piece in enumerate(split3(own * (inv_sq * LOG2E))):
        own_side[16 * i : 16 * i + 16, :] = piece
    own_side[48:64, :] = norm_rows(True, half_norm(own, inv_sq))
    out_ref[...] = jnp.zeros_like(out_ref)

    def step(index, carry):
        data = far_ref.at[index // quarters, index % quarters]
        raw = data[0:16, :]
        for i in range(3):
            far_side[16 * i : 16 * i + 16, :] = raw
        far_side[48:64, :] = norm_rows(False, half_norm(raw.astype(jnp.float32), inv_sq))
        far_rows[...] = far_side[...].T

        def tile(part, total):
            first = pl.multiple_of(part * ROW_TILE, ROW_TILE)
            power = jnp.dot(
                far_rows[pl.ds(first, ROW_TILE), :], own_side[...], preferred_element_type=jnp.float32
            )
            block = jnp.exp2(power).astype(jnp.bfloat16)
            vals = data[16:24, pl.ds(first, ROW_TILE)]
            return total + jnp.dot(vals, block, preferred_element_type=jnp.float32)

        out_ref[...] = lax.fori_loop(0, count // ROW_TILE, tile, out_ref[...])
        return carry

    lax.fori_loop(0, rounds * quarters, step, 0)


def block_product(own, scales, far):
    count = own.shape[1]
    return pl.pallas_call(
        product_kernel,
        out_shape=jax.ShapeDtypeStruct((8, count), jnp.float32),
        scratch_shapes=[
            pltpu.VMEM((DEPTH, count), jnp.bfloat16),
            pltpu.VMEM((DEPTH, count), jnp.bfloat16),
            pltpu.VMEM((count, DEPTH), jnp.bfloat16),
        ],
        compiler_params=pltpu.CompilerParams(vmem_limit_bytes=48 << 20),
    )(own, scales, far)


def move(mask, shard):
    if mask == 0:
        return shard
    return lax.ppermute(shard, "blk", [(i, i ^ mask) for i in range(lax.axis_size("blk"))])


def hop(shard, mask, first_bit, bits):
    index = jnp.bitwise_and(jnp.right_shift(mask, first_bit), (1 << bits) - 1)
    return lax.switch(index, [functools.partial(move, k << first_bit) for k in range(1 << bits)], shard)


def shards(points, values, length_scales, partners):
    bits = lax.axis_size("blk").bit_length() - 1
    near = 3
    round_index = jnp.bitwise_and(lax.axis_index("pair"), 1)
    mask = jnp.bitwise_xor(jnp.where(round_index == 0, partners[0, 0], partners[1, 0]), lax.axis_index("blk"))
    mine = jnp.concatenate([points, values], 0)
    sibling = lax.ppermute(mine, "pair", [(i, i ^ 1) for i in range(lax.axis_size("pair"))])
    far = jnp.stack([mine, sibling])
    far = hop(far, mask, bits - near, near)
    far = hop(far, mask, 0, bits - near)
    far = lax.all_gather(far, "pair", axis=0)
    return block_product(points, length_scales[:, None], far)


def solution(mesh):
    placed = (P(None, ("blk", "pair")), P(None, ("blk", "pair")), P(), P(None, "blk"))
    return jax.shard_map(
        shards, mesh=mesh, in_specs=placed, out_specs=P(None, ("blk", "pair")), check_vma=False
    )
```

```python
import functools
import math

import jax
import jax.numpy as jnp
from jax import lax
from jax.experimental import pallas as pl
from jax.experimental.pallas import tpu as pltpu
from jax.sharding import PartitionSpec as P

LOG2E = math.log2(math.e)
DEPTH = 64
ROW_TILE = 512


def split3(x):
    high = x.astype(jnp.bfloat16)
    rest = x - high.astype(jnp.float32)
    mid = rest.astype(jnp.bfloat16)
    low = (rest - mid.astype(jnp.float32)).astype(jnp.bfloat16)
    return high, mid, low


def half_norm(pts, inv_sq):
    return jnp.sum(pts * pts * inv_sq, axis=0, keepdims=True) * (-0.5 * LOG2E)


def norm_rows(own_first, norm):
    pieces = [p.astype(jnp.float32) for p in split3(norm)]
    row = lax.broadcasted_iota(jnp.int32, (16, norm.shape[1]), 0)
    start = 0 if own_first else 3
    other = 3 - start
    out = jnp.where((row >= other) & (row < other + 3), 1.0, 0.0)
    for i, piece in enumerate(pieces):
        out = jnp.where(row == start + i, piece, out)
    return out.astype(jnp.bfloat16)


def own_rows(points, inv_sq):
    pts = points.astype(jnp.float32)
    pieces = list(split3(pts * (inv_sq * LOG2E)))
    return jnp.concatenate(pieces + [norm_rows(True, half_norm(pts, inv_sq))], 0)


def far_prepare(raw, inv_sq, side, rows):
    for i in range(3):
        side[16 * i : 16 * i + 16, :] = raw
    side[48:64, :] = norm_rows(False, half_norm(raw.astype(jnp.float32), inv_sq))
    rows[...] = side[...].T


def add_unit(total, rows, own_side, vals):
    for first in range(0, rows.shape[0], ROW_TILE):
        part = slice(first, first + ROW_TILE)
        power = jnp.dot(rows[part, :], own_side[...], preferred_element_type=jnp.float32)
        block = jnp.exp2(power).astype(jnp.bfloat16)
        total = total + jnp.dot(vals[:, part], block, preferred_element_type=jnp.float32)
    return total


def product_kernel(scales, own_ref, far_ref, out_ref, own_side, side_a, rows_a, side_b, rows_b):
    units = far_ref.shape[0]
    feature = lax.broadcasted_iota(jnp.int32, (16, 1), 0)
    scale = jnp.ones((16, 1), jnp.float32)
    for i in range(16):
        scale = jnp.where(feature == i, scales[i], scale)
    inv_sq = 1.0 / (scale * scale)
    own_side[...] = own_rows(own_ref[...], inv_sq)
    out_ref[...] = jnp.zeros_like(out_ref)
    far_prepare(far_ref[0, 0:16, :], inv_sq, side_a, rows_a)

    def two_units(pair, carry):
        first = 2 * pair
        far_prepare(far_ref[first + 1, 0:16, :], inv_sq, side_b, rows_b)
        total = add_unit(out_ref[...], rows_a, own_side, far_ref[first, 16:24, :])
        later = lax.rem(first + 2, units)
        far_prepare(far_ref[later, 0:16, :], inv_sq, side_a, rows_a)
        out_ref[...] = add_unit(total, rows_b, own_side, far_ref[first + 1, 16:24, :])
        return carry

    lax.fori_loop(0, units // 2, two_units, 0)


def block_product(own, scales, far):
    count = own.shape[1]
    side = pltpu.VMEM((DEPTH, count), jnp.bfloat16)
    rows = pltpu.VMEM((count, DEPTH), jnp.bfloat16)
    in_vmem = pl.BlockSpec(memory_space=pltpu.VMEM)
    return pl.pallas_call(
        product_kernel,
        out_shape=jax.ShapeDtypeStruct((8, count), jnp.float32),
        in_specs=[pl.BlockSpec(memory_space=pltpu.SMEM), in_vmem, in_vmem],
        out_specs=in_vmem,
        scratch_shapes=[side, side, rows, side, rows],
        compiler_params=pltpu.CompilerParams(vmem_limit_bytes=48 << 20),
    )(scales, own, far)


def move(mask, shard):
    if mask == 0:
        return shard
    return lax.ppermute(shard, "blk", [(i, i ^ mask) for i in range(lax.axis_size("blk"))])


def hop(shard, mask, first_bit, bits):
    index = jnp.bitwise_and(jnp.right_shift(mask, first_bit), (1 << bits) - 1)
    return lax.switch(index, [functools.partial(move, k << first_bit) for k in range(1 << bits)], shard)


def shards(points, values, length_scales, partners):
    bits = lax.axis_size("blk").bit_length() - 1
    near = 3
    round_index = jnp.bitwise_and(lax.axis_index("pair"), 1)
    mask = jnp.bitwise_xor(jnp.where(round_index == 0, partners[0, 0], partners[1, 0]), lax.axis_index("blk"))
    mine = jnp.concatenate([points, values], 0)
    sibling = lax.ppermute(mine, "pair", [(i, i ^ 1) for i in range(lax.axis_size("pair"))])
    far = jnp.stack([mine, sibling])
    far = hop(far, mask, bits - near, near)
    far = hop(far, mask, 0, bits - near)
    far = lax.all_gather(far, "pair", axis=0)
    return block_product(points, length_scales, far.reshape((-1,) + mine.shape))


def solution(mesh):
    placed = (P(None, ("blk", "pair")), P(None, ("blk", "pair")), P(), P(None, "blk"))
    return jax.shard_map(
        shards, mesh=mesh, in_specs=placed, out_specs=P(None, ("blk", "pair")), check_vma=False
    )
```

```python
import functools
import math

import jax
import jax.numpy as jnp
from jax import lax
from jax.experimental import pallas as pl
from jax.experimental.pallas import tpu as pltpu
from jax.sharding import PartitionSpec as P

LOG2E = math.log2(math.e)
DEPTH = 64
ROW_TILE = 512


def split3(x):
    high = x.astype(jnp.bfloat16)
    rest = x - high.astype(jnp.float32)
    mid = rest.astype(jnp.bfloat16)
    low = (rest - mid.astype(jnp.float32)).astype(jnp.bfloat16)
    return high, mid, low


def half_norm(pts, inv_sq):
    return jnp.sum(pts * pts * inv_sq, axis=0, keepdims=True) * (-0.5 * LOG2E)


def norm_rows(own_first, norm):
    pieces = [p.astype(jnp.float32) for p in split3(norm)]
    row = lax.broadcasted_iota(jnp.int32, (16, norm.shape[1]), 0)
    start = 0 if own_first else 3
    other = 3 - start
    out = jnp.where((row >= other) & (row < other + 3), 1.0, 0.0)
    for i, piece in enumerate(pieces):
        out = jnp.where(row == start + i, piece, out)
    return out.astype(jnp.bfloat16)


def own_rows(points, inv_sq):
    pts = points.astype(jnp.float32)
    pieces = list(split3(pts * (inv_sq * LOG2E)))
    return jnp.concatenate(pieces + [norm_rows(True, half_norm(pts, inv_sq))], 0)


def far_prepare(raw, inv_sq, side, rows):
    for i in range(3):
        side[16 * i : 16 * i + 16, :] = raw
    side[48:64, :] = norm_rows(False, half_norm(raw.astype(jnp.float32), inv_sq))
    rows[...] = side[...].T


def add_unit(total, rows, own_side, vals):
    for first in range(0, rows.shape[0], ROW_TILE):
        part = slice(first, first + ROW_TILE)
        power = jnp.dot(rows[part, :], own_side[...], preferred_element_type=jnp.float32)
        block = jnp.exp2(power).astype(jnp.bfloat16)
        total = total + jnp.dot(vals[:, part], block, preferred_element_type=jnp.float32)
    return total


def product_kernel(far_count, chained, *refs):
    scales, own_ref = refs[:2]
    far_refs = refs[2 : 2 + far_count]
    rest = refs[2 + far_count :]
    before, rest = (rest[0], rest[1:]) if chained else (None, rest)
    out_ref, own_side, side_a, rows_a, side_b, rows_b = rest
    feature = lax.broadcasted_iota(jnp.int32, (16, 1), 0)
    scale = jnp.ones((16, 1), jnp.float32)
    for i in range(16):
        scale = jnp.where(feature == i, scales[i], scale)
    inv_sq = 1.0 / (scale * scale)
    own_side[...] = own_rows(own_ref[...], inv_sq)
    units = [(ref, i) for ref in far_refs for i in range(ref.shape[0])]
    slots = [(side_a, rows_a), (side_b, rows_b)]

    def prepare(index):
        ref, i = units[index]
        far_prepare(ref[i, 0:16, :], inv_sq, *slots[index % 2])

    total = before[...] if chained else jnp.zeros(out_ref.shape, jnp.float32)
    prepare(0)
    for index, (ref, i) in enumerate(units):
        if index + 1 < len(units):
            prepare(index + 1)
        total = add_unit(total, slots[index % 2][1], own_side, ref[i, 16:24, :])
    out_ref[...] = total


def block_product(own, scales, far, before=None):
    count = own.shape[1]
    side = pltpu.VMEM((DEPTH, count), jnp.bfloat16)
    rows = pltpu.VMEM((count, DEPTH), jnp.bfloat16)
    in_vmem = pl.BlockSpec(memory_space=pltpu.VMEM)
    chained = before is not None
    operands = [scales, own, *far] + ([before] if chained else [])
    entries = sum(part.shape[0] for part in far) * count * count
    return pl.pallas_call(
        functools.partial(product_kernel, len(far), chained),
        out_shape=jax.ShapeDtypeStruct((8, count), jnp.float32),
        in_specs=[pl.BlockSpec(memory_space=pltpu.SMEM)] + [in_vmem] * (len(operands) - 1),
        out_specs=in_vmem,
        scratch_shapes=[side, side, rows, side, rows],
        cost_estimate=pl.CostEstimate(
            flops=2 * entries * (DEPTH + 8), bytes_accessed=1 << 20, transcendentals=entries
        ),
        compiler_params=pltpu.CompilerParams(vmem_limit_bytes=32 << 20),
    )(*operands)


def swap(shard, offset):
    return lax.ppermute(shard, "pair", [(i, i ^ offset) for i in range(lax.axis_size("pair"))])


def move(mask, shard):
    if mask == 0:
        return shard
    return lax.ppermute(shard, "blk", [(i, i ^ mask) for i in range(lax.axis_size("blk"))])


def hop(shard, mask, first_bit, bits):
    index = jnp.bitwise_and(jnp.right_shift(mask, first_bit), (1 << bits) - 1)
    return lax.switch(index, [functools.partial(move, k << first_bit) for k in range(1 << bits)], shard)


def shards(points, values, length_scales, partners):
    bits = lax.axis_size("blk").bit_length() - 1
    near = 3
    round_index = jnp.bitwise_and(lax.axis_index("pair"), 1)
    mask = jnp.bitwise_xor(jnp.where(round_index == 0, partners[0, 0], partners[1, 0]), lax.axis_index("blk"))
    mine = jnp.concatenate([points, values], 0)
    far = jnp.stack([mine, swap(mine, 1)])
    far = hop(far, mask, bits - near, near)
    far = hop(far, mask, 0, bits - near)
    second = swap(far, 2)
    product = block_product(points, length_scales, [far])
    second, product = lax.optimization_barrier((second, product))
    others = swap(jnp.concatenate([far, second]), 1)
    product = block_product(points, length_scales, [second], product)
    return block_product(points, length_scales, [others], product)


def solution(mesh):
    placed = (P(None, ("blk", "pair")), P(None, ("blk", "pair")), P(), P(None, "blk"))
    return jax.shard_map(
        shards, mesh=mesh, in_specs=placed, out_specs=P(None, ("blk", "pair")), check_vma=False
    )
```

```python
import functools
import math

import jax
import jax.numpy as jnp
from jax import lax
from jax.experimental import pallas as pl
from jax.experimental.pallas import tpu as pltpu
from jax.sharding import PartitionSpec as P

LOG2E = math.log2(math.e)
DEPTH = 64
ROW_TILE = 512


def split3(x):
    high = x.astype(jnp.bfloat16)
    rest = x - high.astype(jnp.float32)
    mid = rest.astype(jnp.bfloat16)
    low = (rest - mid.astype(jnp.float32)).astype(jnp.bfloat16)
    return high, mid, low


def half_norm(pts, inv_sq):
    return jnp.sum(pts * pts * inv_sq, axis=0, keepdims=True) * (-0.5 * LOG2E)


def norm_rows(own_first, norm):
    pieces = [p.astype(jnp.float32) for p in split3(norm)]
    row = lax.broadcasted_iota(jnp.int32, (16, norm.shape[1]), 0)
    start = 0 if own_first else 3
    other = 3 - start
    out = jnp.where((row >= other) & (row < other + 3), 1.0, 0.0)
    for i, piece in enumerate(pieces):
        out = jnp.where(row == start + i, piece, out)
    return out.astype(jnp.bfloat16)


def own_rows(points, inv_sq):
    pts = points.astype(jnp.float32)
    pieces = list(split3(pts * (inv_sq * LOG2E)))
    return jnp.concatenate(pieces + [norm_rows(True, half_norm(pts, inv_sq))], 0)


def far_prepare(raw, inv_sq, side, rows):
    for i in range(3):
        side[16 * i : 16 * i + 16, :] = raw
    side[48:64, :] = norm_rows(False, half_norm(raw.astype(jnp.float32), inv_sq))
    rows[...] = side[...].T


def add_unit(total, rows, own_side, vals):
    for first in range(0, rows.shape[0], ROW_TILE):
        part = slice(first, first + ROW_TILE)
        power = jnp.dot(rows[part, :], own_side[...], preferred_element_type=jnp.float32)
        block = jnp.exp2(power).astype(jnp.bfloat16)
        total = total + jnp.dot(vals[:, part], block, preferred_element_type=jnp.float32)
    return total


def product_kernel(far_count, chained, *refs):
    scales, own_ref = refs[:2]
    far_refs = refs[2 : 2 + far_count]
    rest = refs[2 + far_count :]
    before, rest = (rest[0], rest[1:]) if chained else (None, rest)
    out_ref, own_side, side_a, rows_a, side_b, rows_b = rest
    feature = lax.broadcasted_iota(jnp.int32, (16, 1), 0)
    scale = jnp.ones((16, 1), jnp.float32)
    for i in range(16):
        scale = jnp.where(feature == i, scales[i], scale)
    inv_sq = 1.0 / (scale * scale)
    own_side[...] = own_rows(own_ref[...], inv_sq)
    units = [(ref, i) for ref in far_refs for i in range(ref.shape[0])]
    slots = [(side_a, rows_a), (side_b, rows_b)]

    def prepare(index):
        ref, i = units[index]
        far_prepare(ref[i, 0:16, :], inv_sq, *slots[index % 2])

    total = before[...] if chained else jnp.zeros(out_ref.shape, jnp.float32)
    prepare(0)
    for index, (ref, i) in enumerate(units):
        if index + 1 < len(units):
            prepare(index + 1)
        total = add_unit(total, slots[index % 2][1], own_side, ref[i, 16:24, :])
    out_ref[...] = total


def block_product(own, scales, far, before=None):
    count = own.shape[1]
    side = pltpu.VMEM((DEPTH, count), jnp.bfloat16)
    rows = pltpu.VMEM((count, DEPTH), jnp.bfloat16)
    in_vmem = pl.BlockSpec(memory_space=pltpu.VMEM)
    chained = before is not None
    operands = [scales, own, *far] + ([before] if chained else [])
    entries = sum(part.shape[0] for part in far) * count * count
    return pl.pallas_call(
        functools.partial(product_kernel, len(far), chained),
        out_shape=jax.ShapeDtypeStruct((8, count), jnp.float32),
        in_specs=[pl.BlockSpec(memory_space=pltpu.SMEM)] + [in_vmem] * (len(operands) - 1),
        out_specs=in_vmem,
        scratch_shapes=[side, side, rows, side, rows],
        cost_estimate=pl.CostEstimate(
            flops=2 * entries * (DEPTH + 8), bytes_accessed=1 << 20, transcendentals=entries
        ),
        compiler_params=pltpu.CompilerParams(vmem_limit_bytes=32 << 20),
    )(*operands)


def swap(shard, offset):
    return lax.ppermute(shard, "pair", [(i, i ^ offset) for i in range(lax.axis_size("pair"))])


def move(mask, shard):
    if mask == 0:
        return shard
    return lax.ppermute(shard, "blk", [(i, i ^ mask) for i in range(lax.axis_size("blk"))])


def hop(shard, mask, first_bit, bits):
    index = jnp.bitwise_and(jnp.right_shift(mask, first_bit), (1 << bits) - 1)
    return lax.switch(index, [functools.partial(move, k << first_bit) for k in range(1 << bits)], shard)


def shards(points, values, length_scales, partners):
    bits = lax.axis_size("blk").bit_length() - 1
    near = 3
    round_index = jnp.bitwise_and(lax.axis_index("pair"), 1)
    partner = lax.dynamic_index_in_dim(partners[:, 0], round_index, 0, keepdims=False)
    mask = jnp.bitwise_xor(partner, lax.axis_index("blk"))
    mine = jnp.concatenate([points, values], 0)
    far = jnp.stack([mine, swap(mine, 1)])
    far = hop(far, mask, bits - near, near)
    far = hop(far, mask, 0, bits - near)
    second = swap(far, 2)
    product = block_product(points, length_scales, [far])
    second, product = lax.optimization_barrier((second, product))
    others = swap(jnp.concatenate([far, second]), 1)
    product = block_product(points, length_scales, [second], product)
    return block_product(points, length_scales, [others], product)


def solution(mesh):
    placed = (P(None, ("blk", "pair")), P(None, ("blk", "pair")), P(), P(None, "blk"))
    return jax.shard_map(
        shards, mesh=mesh, in_specs=placed, out_specs=P(None, ("blk", "pair")), check_vma=False
    )
```
